256 devices in a mesh: dp: 16 (over z_lo, y), seq: 16 (over z_hi, x, core).
Axes of the slice: x: 4, y: 4, z: 8 (z_hi: 2, z_lo: 4; z = z_hi * 4 + z_lo), core: 2. Of those that a mesh axis runs over, the one named last changes fastest.
Arguments:
- track: bfloat16 [98304, 1280], P(('dp', 'seq')), parts along dimension 0, may hold values from -6 to 6
- conv_weight: bfloat16 [1536, 5, 1280], P('seq'), may hold values from -0.078125 to 0.078125
- qkv_weight: bfloat16 [1344, 1536], P('seq'), may hold values from -16 to 16
- out_weight: bfloat16 [1536, 1536], P('seq'), may hold values from -0.15625 to 0.15625
Outputs:
- mixed: bfloat16 [49152, 1536], P(('dp', 'seq')), parts along dimension 0
The draws below stay inside these ranges and needn't reach their ends.
There are 16 independent parts, one for each index of `dp`. The reference program is written for one: setup_inputs(seed, part) draws one part's arguments, and reference() takes and returns one part's arrays. A program takes and returns all parts, laid end to end along the dimension named above; an argument that names none is the same for every part. Nothing has to cross between parts.
All inputs are finite; a program needn't handle non-finite values.
Results may differ from the reference program's by a relative error of at most 0.015.
The reference program's roundings to bfloat16 on the way count: a program that leaves them out, or rounds other values in their place, can miss the bound.
Values may be sent and summed in bfloat16 or wider, within the bound.
No kernel may reach another device: no remote copies, remote signals or barrier semaphores. Data moves between devices by JAX's collectives and lax.ppermute only.
A program may use at most 128 MiB of HBM per device.

```python
import math
import jax
import jax.numpy as jnp
from jax import lax

C_IN = 1280
C = 1536
HEADS = 8
QK = 128
VD = 192
KW = 5
TOKENS = 3072
POSITIONS = 6144


def draw_qkv_weight(key, part):
    key = jax.random.fold_in(key, 7)
    base_key, head_key = jax.random.split(key)
    base = jax.random.uniform(base_key, (HEADS * QK + QK + VD, C), jnp.float32, -math.sqrt(3.0), math.sqrt(3.0)) / math.sqrt(C)
    factors = jnp.exp(jax.random.uniform(head_key, (HEADS,), jnp.float32, 0.0, math.log(4.0)))
    row_scale = jnp.concatenate([jnp.repeat(factors, QK), jnp.ones((QK + VD,), jnp.float32)])
    return (base * row_scale[:, None]).astype(jnp.bfloat16)


def block_scale(own_key, shape, shards, low, largest):
    def one(position, blocks):
        heights = jax.random.uniform(jax.random.fold_in(jax.random.fold_in(own_key, 6), position), (blocks,), jnp.float32, low / len(shards), largest / len(shards))
        return jnp.repeat(jnp.exp(heights), shape[position] // blocks).reshape((-1,) + (1,) * (len(shape) - position - 1))

    loudness = one(*shards[0])
    for cut in shards[1:]:
        loudness = loudness * one(*cut)
    return loudness


def noise(rng, extent, width, most, cuts=(), dtype=jnp.bfloat16):
    result = width * jax.random.normal(rng, extent, jnp.float32)
    if cuts:
        result = result * block_scale(rng, extent, cuts, -0.22, 0.18)
    return jnp.clip(result, -most, most).astype(dtype)


def setup_inputs(seed: int = 0, part: int = 0) -> dict:
    key_of = jax.random.split(jax.random.key(seed), 5)
    part_keys = jax.random.split(jax.random.fold_in(key_of[4], part), 5)
    return {
        "track": noise(part_keys[0], (POSITIONS, C_IN), 1.0, 6.0, ((0, 16),)),
        "conv_weight": noise(key_of[1], (C, KW, C_IN), (KW * C_IN) ** -0.5, 0.078125, ((0, 16),)),
        "qkv_weight": draw_qkv_weight(jax.random.fold_in(key_of[4], 71), part),
        "out_weight": noise(key_of[3], (C, HEADS * VD), (HEADS * VD) ** -0.5, 0.15625, ((0, 16),)),
    }


epsilon = 1e-06

def rms_scaled(values):
    return values * lax.rsqrt(lax.optimization_barrier(jnp.mean(values * values, axis=-1, keepdims=True)) + epsilon)

def contract_last(left, right):
    return lax.dot_general(left, right, (((1,), (1,)), ((), ())), preferred_element_type=jnp.float32)

def reference(track, conv_weight, qkv_weight, out_weight):
    activated = jax.nn.gelu(rms_scaled(track.astype(jnp.float32))).astype(jnp.bfloat16)
    padded = jnp.pad(activated, ((2, 2), (0, 0)))
    convolved = jnp.zeros((POSITIONS, C), jnp.float32)
    for offset in range(KW):
        convolved = convolved + contract_last(padded[offset:offset + POSITIONS], conv_weight[:, offset, :])
    pooled = lax.optimization_barrier(jnp.max(convolved.reshape(TOKENS, 2, C), axis=1)).astype(jnp.bfloat16)
    normed = rms_scaled(pooled.astype(jnp.float32)).astype(jnp.bfloat16)
    projected = contract_last(normed, qkv_weight).astype(jnp.bfloat16)
    queries = projected[:, :HEADS * QK].reshape(TOKENS, HEADS, QK).transpose(1, 0, 2)
    key_rows = projected[:, HEADS * QK:HEADS * QK + QK]
    value_rows = projected[:, HEADS * QK + QK:]
    scaling = QK ** (-0.5)

    def one_head(query_block):
        scores = jnp.dot(query_block, key_rows.T, preferred_element_type=jnp.float32) * scaling
        top = lax.optimization_barrier(jnp.max(scores, axis=1, keepdims=True))
        expo = jnp.exp(scores - top)
        total = lax.optimization_barrier(jnp.sum(expo, axis=1, keepdims=True))
        return jnp.dot(expo.astype(jnp.bfloat16), value_rows, preferred_element_type=jnp.float32) / total
    heads = lax.map(one_head, queries)
    heads = heads.transpose(1, 0, 2).reshape(TOKENS, HEADS * VD).astype(jnp.bfloat16)
    mixed = pooled.astype(jnp.float32) + contract_last(heads, out_weight)
    return mixed.astype(jnp.bfloat16)
```

```python
import functools

import jax
import jax.numpy as jnp
from jax import lax
from jax.experimental import pallas as pl
from jax.experimental.pallas import tpu as pltpu
from jax.sharding import PartitionSpec as P

HEADS = 8
QK = 128
VD = 192
EPS = 1e-06
AXES = ("dp", "seq")
MIB = 1024 * 1024
NT = (((1,), (1,)), ((), ()))


def spot(x, y, z, core):
    return ((z % 4) * 4 + y) * 16 + (z // 4) * 8 + x * 2 + core


def route(move):
    pairs = []
    for z in range(8):
        for y in range(4):
            for x in range(4):
                for core in range(2):
                    a, b, c, d = move(x, y, z, core)
                    pairs.append((spot(x, y, z, core), spot(a % 4, b % 4, c % 8, d % 2)))
    return pairs


def send(value, move):
    return lax.ppermute(value, AXES, route(move))


def sign(core):
    return 1 - 2 * core


def call(body, out, scratch=(), flops=0, name=None, specs=None):
    extra = {} if specs is None else {"in_specs": specs}
    return pl.pallas_call(
        body,
        out_shape=out,
        scratch_shapes=list(scratch),
        compiler_params=pltpu.CompilerParams(vmem_limit_bytes=48 * MIB),
        cost_estimate=pl.CostEstimate(flops=flops, bytes_accessed=2 * MIB, transcendentals=0),
        name=name,
        **extra,
    )


def bf16(*shape):
    return jax.ShapeDtypeStruct(shape, jnp.bfloat16)


def f32(*shape):
    return jax.ShapeDtypeStruct(shape, jnp.float32)


def rms_scaled(values):
    return values * lax.rsqrt(jnp.mean(values * values, axis=-1, keepdims=True) + EPS)


def gelu_rows(values):
    return jax.nn.gelu(rms_scaled(values.astype(jnp.float32)))


def gelu_kernel(track, top, bottom, out):
    for i in range(6):
        rows = slice(i * 64, i * 64 + 64)
        out[rows, :] = gelu_rows(track[rows, :]).astype(jnp.bfloat16)
    edge = jnp.concatenate([gelu_rows(top[...]), gelu_rows(bottom[...])], axis=0)
    out[384:400, :] = edge.astype(jnp.bfloat16)


def conv_tile(act, weight, flat, shifted):
    for c in range(10):
        cols = slice(c * 128, (c + 1) * 128)
        flat[c, 8:392, :] = act[0:384, cols].astype(jnp.float32)
        edge = act[384:400, cols].astype(jnp.float32)
        flat[c, 0:8, :] = edge[0:8]
        flat[c, 392:400, :] = edge[8:16]
        for j in range(6):
            shifted[j * 192 : (j + 1) * 192, cols] = flat[c, pl.ds(6 + j, 192, stride=2), :].astype(jnp.bfloat16)
    total = jnp.zeros((384, weight.shape[1]), jnp.float32)
    for k in range(5):
        total = total + lax.dot_general(
            shifted[k * 192 : (k + 2) * 192, :], weight[k], NT, preferred_element_type=jnp.float32
        )
    return jnp.maximum(total[0:192], total[192:384]).astype(jnp.bfloat16)


def conv_first(act, weight, out, flat, shifted):
    out[...] = conv_tile(act, weight, flat, shifted)


def conv_second(act, weight, first, out, flat, shifted):
    out[:, 0:192] = first[...]
    out[:, 192:384] = conv_tile(act, weight, flat, shifted)


CONV_SCRATCH = (pltpu.VMEM((10, 400, 128), jnp.float32), pltpu.VMEM((1152, 1280), jnp.bfloat16))


def conv_a(act, weight):
    return call(conv_first, bf16(192, 192), CONV_SCRATCH, 2 * 384 * 6400 * 192, "conv_a")(act, weight)


def conv_b(act, weight, first):
    return call(conv_second, bf16(192, 384), CONV_SCRATCH, 2 * 384 * 6400 * 192, "conv_b")(act, weight, first)


def shards_dot(spots, columns, pieces, blocks):
    x, y, zh, c = spots[0], spots[1], spots[2], spots[3]
    quarter = [y, (y + 3) % 4, (y + 1) % 4, (y + 2) % 4]
    column = [x, (x + 3) % 4, (x + 1) % 4, (x + 2) % 4]
    for side in range(2):
        total = jnp.zeros((192, 768), jnp.float32)
        for r in range(4):
            weight = pieces[side * 4 + r][...].reshape(768, 384)
            total = total + lax.dot_general(
                columns[quarter[r]], weight, NT, preferred_element_type=jnp.float32
            )
        for zr in range(2):
            for xr in range(4):
                t = zr * 4 + xr
                index = ((zh + zr) % 2) * 8 + column[xr] * 2 + (c + side) % 2
                blocks[index] = total[:, t * 96 : t * 96 + 96]


def project_kernel(spots, p0, p1, p2, p3, w0, w1, w2, w3, w4, w5, w6, w7, pooled, q_out, kv_out, tiles, columns, blocks, wide):
    x, zh, c = spots[0], spots[2], spots[3]
    step = 1 - 2 * c
    for s, piece in enumerate((p0, p1, p2, p3)):
        home = (x + s * step + 4) % 4
        tiles[zh * 4 + home] = piece[:, 0:192]
        tiles[(1 - zh) * 4 + home] = piece[:, 192:384]
    for i in range(8):
        pooled[:, i * 192 : i * 192 + 192] = tiles[i]
    normed = rms_scaled(pooled[...].astype(jnp.float32)).astype(jnp.bfloat16)
    for i in range(4):
        columns[i] = normed[:, i * 384 : i * 384 + 384]
    shards_dot(spots, columns, (w0, w1, w2, w3, w4, w5, w6, w7), blocks)
    for i in range(16):
        wide[:, i * 84 : i * 84 + 84] = blocks[i][:, 0:84].astype(jnp.bfloat16)
    q_out[...] = wide[:, 0 : HEADS * QK]
    kv_out[...] = wide[:, HEADS * QK : HEADS * QK + QK + VD]


def smem():
    return pl.BlockSpec(memory_space=pltpu.SMEM)


def vmem():
    return pl.BlockSpec(memory_space=pltpu.VMEM)


def project(spots, tiles, pieces):
    return call(
        project_kernel,
        (bf16(192, 1536), bf16(192, 1024), bf16(192, 320)),
        (
            pltpu.VMEM((8, 192, 192), jnp.bfloat16),
            pltpu.VMEM((4, 192, 384), jnp.bfloat16),
            pltpu.VMEM((16, 192, 96), jnp.float32),
            pltpu.VMEM((192, 1344), jnp.bfloat16),
        ),
        2 * 192 * 1536 * 1536,
        "project",
        [smem()] + [vmem()] * 12,
    )(spots, *tiles, *pieces)


SCALE = QK ** (-0.5) * 1.4426950408889634


def attend(q, own, sibling, h, state):
    query = q[:, h * QK : (h + 1) * QK]
    blocks = [own[...].reshape(768, 320), sibling[...].reshape(768, 320)]
    scores = [
        lax.dot_general(query, b[:, 0:QK], NT, preferred_element_type=jnp.float32) for b in blocks
    ]
    top = jnp.maximum(
        jnp.max(scores[0], axis=1, keepdims=True), jnp.max(scores[1], axis=1, keepdims=True)
    )
    if state is not None:
        top = jnp.maximum(top, state[0])
    shift = top * SCALE
    expo = [jnp.exp2(s * SCALE - shift) for s in scores]
    total = jnp.sum(expo[0], axis=1, keepdims=True) + jnp.sum(expo[1], axis=1, keepdims=True)
    value = jnp.dot(expo[0].astype(jnp.bfloat16), blocks[0][:, QK:], preferred_element_type=jnp.float32)
    value = value + jnp.dot(
        expo[1].astype(jnp.bfloat16), blocks[1][:, QK:], preferred_element_type=jnp.float32
    )
    if state is not None:
        factor = jnp.exp2(state[0] * SCALE - shift)
        total = total + state[1] * factor
        value = value + state[2] * factor
    return top, total, value


def attend_first(q, own, sibling, top_out, total_out, value_out):
    for h in range(HEADS):
        top, total, value = attend(q, own, sibling, h, None)
        top_out[:, h : h + 1] = top
        total_out[:, h : h + 1] = total
        value_out[h] = value


def attend_second(q, own, sibling, top_in, total_in, value_in, heads):
    for h in range(HEADS):
        state = (top_in[:, h : h + 1], total_in[:, h : h + 1], value_in[h])
        top, total, value = attend(q, own, sibling, h, state)
        heads[:, h * VD : (h + 1) * VD] = (value / total).astype(jnp.bfloat16)


ATTEND_FLOPS = 2 * 192 * 8 * 1536 * 320


def output_kernel(spots, heads, pooled, w0, w1, w2, w3, w4, w5, w6, w7, mixed, columns, blocks, wide):
    for i in range(4):
        columns[i] = heads[:, i * 384 : i * 384 + 384]
    shards_dot(spots, columns, (w0, w1, w2, w3, w4, w5, w6, w7), blocks)
    for i in range(16):
        wide[:, i * 96 : i * 96 + 96] = blocks[i]
    mixed[...] = (pooled[...].astype(jnp.float32) + wide[...]).astype(jnp.bfloat16)


def output(spots, heads, pooled, pieces):
    return call(
        output_kernel,
        bf16(192, 1536),
        (
            pltpu.VMEM((4, 192, 384), jnp.bfloat16),
            pltpu.VMEM((16, 192, 96), jnp.float32),
            pltpu.VMEM((192, 1536), jnp.float32),
        ),
        2 * 192 * 1536 * 1536,
        "output",
        [smem()] + [vmem()] * 10,
    )(spots, heads, pooled, *pieces)


def ring4(value, core, axis):
    if axis == "x":
        before = send(value, lambda x, y, z, c: (x + 1, y, z, c))
        after = send(value, lambda x, y, z, c: (x - 1, y, z, c))
        far = send(
            jnp.where(core == 0, before, after), lambda x, y, z, c: (x + sign(c), y, z, c)
        )
    else:
        before = send(value, lambda x, y, z, c: (x, y + 1, z, c))
        after = send(value, lambda x, y, z, c: (x, y - 1, z, c))
        far = send(
            jnp.where(core == 0, before, after), lambda x, y, z, c: (x, y + sign(c), z, c)
        )
    return [value, before, after, far]


def swap(value):
    return send(value, lambda x, y, z, c: (x, y, z, 1 - c))


def across(value):
    return send(value, lambda x, y, z, c: (x, y, z + 4, c))


def by_core(core, own, sibling):
    low = jnp.where(core == 0, own, sibling).reshape(5, 96, 1280)
    high = jnp.where(core == 0, sibling, own).reshape(5, 96, 1280)
    return jnp.concatenate([low, high], axis=1)


def on_device(track, conv_weight, qkv_weight, out_weight):
    dp = lax.axis_index("dp")
    seq = lax.axis_index("seq")
    x, y, zh, core = (seq // 2) % 4, dp % 4, seq // 8, seq % 2
    spots = jnp.stack([x, y, zh, core]).astype(jnp.int32)

    top = lax.ppermute(track[376:384], "seq", [(i, i + 1) for i in range(15)])
    bottom = lax.ppermute(track[0:8], "seq", [(i + 1, i) for i in range(15)])
    act = call(gelu_kernel, bf16(400, 1280), name="gelu")(track, top, bottom)
    blocks = [act]
    for _ in range(3):
        blocks.append(send(blocks[-1], lambda x, y, z, c: (x + sign(c), y, z, c)))

    own = jnp.transpose(conv_weight, (1, 0, 2)).reshape(480, 1280)
    weight_a = by_core(core, own, swap(own))
    crossed = across(lax.dynamic_slice(own, (120 * y, 0), (120, 1280)))
    parts = ring4(crossed, core, "y")
    other = jnp.zeros((4, 120, 1280), jnp.bfloat16)
    for part, place in zip(parts, (y, (y + 3) % 4, (y + 1) % 4, (y + 2) % 4)):
        other = lax.dynamic_update_slice(other, part[None], (place, 0, 0))
    other = other.reshape(480, 1280)
    weight_b = by_core(core, other, swap(other))

    padded = jnp.concatenate([qkv_weight, jnp.zeros((12, 1536), jnp.bfloat16), out_weight], axis=0)
    quarter = lax.dynamic_slice(padded, (0, 384 * y), (192, 384))
    near = jnp.stack(ring4(quarter, core, "x"))
    pieces = []
    for rows in (slice(0, 96), slice(96, 192)):
        half = near[:, rows]
        types = jnp.concatenate([half, across(half)], axis=0)
        gathered = jnp.stack(ring4(types, core, "y"))
        sibling = swap(gathered)
        pieces.append([gathered[r] for r in range(4)] + [sibling[r] for r in range(4)])

    tiles = []
    for s in range(4):
        tile = conv_b(blocks[s], weight_b, conv_a(blocks[s], weight_a))
        if s:
            tile = send(tile, lambda x, y, z, c, s=s: (x - s * sign(c), y, z, c))
        tiles.append(tile)
    pooled, queries, kv = project(spots, tiles, pieces[0])

    def spread(block):
        near = [block] + [
            send(block, lambda x, y, z, c, s=s: (x + s, y, z, c)) for s in (1, 3, 2)
        ]
        mine = jnp.stack(near)
        return mine, swap(mine)

    near_own, near_sibling = spread(kv)
    far_own, far_sibling = spread(across(kv))
    state = call(
        attend_first, (f32(192, 8), f32(192, 8), f32(8, 192, 192)), flops=ATTEND_FLOPS, name="attend_first"
    )(queries, near_own, near_sibling)
    heads = call(attend_second, bf16(192, 1536), flops=ATTEND_FLOPS, name="attend_second")(
        queries, far_own, far_sibling, *state
    )
    return output(spots, heads, pooled, pieces[1])


def solution(mesh):
    return jax.shard_map(
        on_device,
        mesh=mesh,
        in_specs=(P(("dp", "seq"), None), P("seq", None, None), P("seq", None), P("seq", None)),
        out_specs=P(("dp", "seq"), None),
        check_vma=False,
    )
```

```python
import functools

import jax
import jax.numpy as jnp
from jax import lax
from jax.experimental import pallas as pl
from jax.experimental.pallas import tpu as pltpu
from jax.sharding import PartitionSpec as P

HEADS = 8
QK = 128
VD = 192
EPS = 1e-06
AXES = ("dp", "seq")
MIB = 1024 * 1024
NT = (((1,), (1,)), ((), ()))


def spot(x, y, z, core):
    return ((z % 4) * 4 + y) * 16 + (z // 4) * 8 + x * 2 + core


def route(move):
    pairs = []
    for z in range(8):
        for y in range(4):
            for x in range(4):
                for core in range(2):
                    a, b, c, d = move(x, y, z, core)
                    pairs.append((spot(x, y, z, core), spot(a % 4, b % 4, c % 8, d % 2)))
    return pairs


def send(value, move):
    return lax.ppermute(value, AXES, route(move))


def call(body, out, scratch=(), flops=0, name=None, specs=None):
    extra = {} if specs is None else {"in_specs": specs}
    return pl.pallas_call(
        body,
        out_shape=out,
        scratch_shapes=list(scratch),
        compiler_params=pltpu.CompilerParams(vmem_limit_bytes=24 * MIB),
        cost_estimate=pl.CostEstimate(flops=0, bytes_accessed=0, transcendentals=0),
        name=name,
        **extra,
    )


def bf16(*shape):
    return jax.ShapeDtypeStruct(shape, jnp.bfloat16)


def f32(*shape):
    return jax.ShapeDtypeStruct(shape, jnp.float32)


def rms_scaled(values):
    return values * lax.rsqrt(jnp.mean(values * values, axis=-1, keepdims=True) + EPS)


def gelu_rows(values):
    return jax.nn.gelu(rms_scaled(values.astype(jnp.float32)))


def pack_kernel(spots, conv, qkv, out, packed):
    packed[0:64, 1152:1280] = jnp.zeros((64, 128), jnp.bfloat16)
    packed[0:32, 768:1152] = jnp.zeros((32, 384), jnp.bfloat16)
    for i in range(3):
        rows = min(32, 84 - 32 * i)
        packed[0:rows, i * 384 : i * 384 + 384] = qkv[32 * i : 32 * i + rows, :]
        packed[32:64, i * 384 : i * 384 + 384] = out[32 * i : 32 * i + 32, :]
    packed[64:184, :] = conv[0]


def pack(spots, conv, qkv, out):
    return pl.pallas_call(
        pack_kernel,
        grid_spec=pltpu.PrefetchScalarGridSpec(
            num_scalar_prefetch=1,
            grid=(1,),
            in_specs=[
                pl.BlockSpec((1, 120, 1280), lambda i, spots: (spots[22], 0, 0)),
                pl.BlockSpec((84, 384), lambda i, spots: (0, spots[14])),
                pl.BlockSpec((96, 384), lambda i, spots: (0, spots[22])),
            ],
            out_specs=pl.BlockSpec((184, 1280), lambda i, spots: (0, 0)),
        ),
        out_shape=bf16(184, 1280),
        name="pack",
    )(spots, conv, qkv, out)


def gelu_kernel(track, edges, out):
    for i in range(0, 384, 48):
        out[i : i + 48, :] = gelu_rows(track[i : i + 48, :]).astype(jnp.bfloat16)
    out[384:400, :] = gelu_rows(edges[...]).astype(jnp.bfloat16)


def gelu(track, edges):
    return call(gelu_kernel, bf16(400, 1280), name="gelu")(track, edges)


def conv_tile(act, weight, flat, shifted):
    for c in range(10):
        cols = slice(c * 128, (c + 1) * 128)
        flat[c, 8:392, :] = act[0:384, cols].astype(jnp.float32)
        edge = act[384:400, cols].astype(jnp.float32)
        flat[c, 0:8, :] = edge[0:8]
        flat[c, 392:400, :] = edge[8:16]
        for j in range(6):
            shifted[j * 192 : (j + 1) * 192, cols] = flat[c, pl.ds(6 + j, 192, stride=2), :].astype(jnp.bfloat16)
    total = jnp.zeros((384, weight.shape[1]), jnp.float32)
    for k in range(5):
        total = total + lax.dot_general(
            shifted[k * 192 : (k + 2) * 192, :], weight[k], NT, preferred_element_type=jnp.float32
        )
    return jnp.maximum(total[0:192], total[192:384]).astype(jnp.bfloat16)


def conv_first(act, weight, out, flat, shifted):
    out[...] = conv_tile(act, weight, flat, shifted)


def conv_second(act, weight, first, out, flat, shifted):
    out[:, 0:192] = first[...]
    out[:, 192:384] = conv_tile(act, weight, flat, shifted)


CONV_SCRATCH = (pltpu.VMEM((10, 400, 128), jnp.float32), pltpu.VMEM((1152, 1280), jnp.bfloat16))


def conv_a(act, weight):
    return call(conv_first, bf16(192, 192), CONV_SCRATCH, 2 * 384 * 6400 * 192, "conv_a")(act, weight)


def conv_b(act, weight, first):
    return call(conv_second, bf16(192, 384), CONV_SCRATCH, 2 * 384 * 6400 * 192, "conv_b")(act, weight, first)


def spots_of(x, y, z_low, zh, core):
    def listed(v, c):
        one, three = v ^ 1, v ^ 3
        return [v, jnp.where(c == 0, one, three), jnp.where(c == 0, three, one), v ^ 2]

    def place(c):
        found = []
        for a in range(4):
            d = x ^ a
            near = jnp.where(d == 1, 1 + c, 2 - c)
            found.append(jnp.where(d == 0, 0, jnp.where(d == 2, 3, near)))
        return found

    values = [zh, core] + listed(x, core) + place(core) + place(1 - core)
    for v in (z_low, y):
        values += listed(v, core) + listed(v, 1 - core)
    return jnp.stack(values).astype(jnp.int32)


def smem():
    return pl.BlockSpec(memory_space=pltpu.SMEM)


def vmem():
    return pl.BlockSpec(memory_space=pltpu.VMEM)


def place_kernel(spots, own0, own1, sib0, sib1, out, rows):
    core = spots[1]
    for side, pair in enumerate(((own0, own1), (sib0, sib1))):
        which = (core + side) % 2
        for r in range(4):
            quarter = spots[22 + 4 * side + r]
            rows[which * 4 + quarter] = pair[r // 2][r % 2]
    for c in range(2):
        whole = jnp.concatenate([rows[c * 4 + q] for q in range(4)], axis=0)
        for k in range(5):
            out[k, c * 96 : (c + 1) * 96, :] = whole[k * 96 : (k + 1) * 96]


def place(spots, own, sibling):
    return call(
        place_kernel,
        bf16(5, 192, 1280),
        (pltpu.VMEM((8, 120, 1280), jnp.bfloat16),),
        0,
        "place",
        [smem()] + [vmem()] * 4,
    )(spots, *own, *sibling)


def key_value_kernel(spots, p0, p1, p2, p3, a0, a1, b0, b1, pooled, columns, kv, tiles, wide):
    zh, core = spots[0], spots[1]
    for s, piece in enumerate((p0, p1, p2, p3)):
        home = spots[2 + s]
        tiles[zh * 4 + home] = piece[:, 0:192]
        tiles[(1 - zh) * 4 + home] = piece[:, 192:384]
    for i in range(8):
        pooled[:, i * 192 : i * 192 + 192] = tiles[i]
    normed = rms_scaled(pooled[...].astype(jnp.float32)).astype(jnp.bfloat16)
    for i in range(4):
        columns[i] = normed[:, i * 384 : i * 384 + 384]
    for i in range(4):
        x, c = 2 + i // 2, i % 2
        total = jnp.zeros((192, 96), jnp.float32)
        for r in range(4):
            t = jnp.where(core == c, spots[6 + x], spots[10 + x])
            own = (a0, a1)[r // 2][r % 2, t, 1]
            sibling = (b0, b1)[r // 2][r % 2, t, 1]
            weight = jnp.where(core == c, own, sibling)
            quarter = jnp.where(core == c, spots[14 + r], spots[18 + r])
            total = total + lax.dot_general(
                columns[quarter], weight, NT, preferred_element_type=jnp.float32
            )
        wide[:, i * 84 : i * 84 + 84] = total[:, 0:84]
    kv[...] = wide[:, 16:336].astype(jnp.bfloat16)


def key_value(spots, tiles, own, sibling):
    return call(
        key_value_kernel,
        (bf16(192, 1536), bf16(4, 192, 384), bf16(192, 320)),
        (pltpu.VMEM((8, 192, 192), jnp.bfloat16), pltpu.VMEM((192, 336), jnp.float32)),
        2 * 192 * 1536 * 384,
        "key_value",
        [smem()] + [vmem()] * 8,
    )(spots, *tiles, *own, *sibling)


def spread_blocks(spots, side, total, blocks):
    for x in range(4):
        home = spots[2 + x] if side == 0 else spots[2 + (0, 2, 1, 3)[x]]
        for zh in range(2):
            t = x * 2 + zh
            blocks[zh * 8 + home * 2 + (spots[1] + side) % 2] = total[:, t * 96 : t * 96 + 96]


def shards_dot(spots, base, columns, pairs, blocks):
    for side in range(2):
        total = jnp.zeros((192, 768), jnp.float32)
        for r in range(4):
            weight = pairs[side][r // 2][r % 2].reshape(768, 384)
            total = total + lax.dot_general(
                columns[spots[base + 4 * side + r]], weight, NT, preferred_element_type=jnp.float32
            )
        spread_blocks(spots, side, total, blocks)


def query_kernel(spots, columns, a0, a1, b0, b1, q, blocks, wide):
    shards_dot(spots, 14, columns, ((a0, a1), (b0, b1)), blocks)
    for i in range(13):
        wide[:, i * 84 : i * 84 + 84] = blocks[i][:, 0:84]
    q[...] = wide[:, 0 : HEADS * QK].astype(jnp.bfloat16)


def query(spots, columns, own, sibling):
    return call(
        query_kernel,
        bf16(192, 1024),
        (pltpu.VMEM((16, 192, 96), jnp.float32), pltpu.VMEM((192, 1092), jnp.float32)),
        2 * 192 * 1536 * 1536,
        "query",
        [smem()] + [vmem()] * 5,
    )(spots, columns, *own, *sibling)


SCALE = QK ** (-0.5) * 1.4426950408889634


def attend(q, own, sibling, h, state):
    query = q[:, h * QK : (h + 1) * QK]
    blocks = [own[...].reshape(768, 320), sibling[...].reshape(768, 320)]
    scores = [
        lax.dot_general(query, b[:, 0:QK], NT, preferred_element_type=jnp.float32) for b in blocks
    ]
    top = jnp.maximum(
        jnp.max(scores[0], axis=1, keepdims=True), jnp.max(scores[1], axis=1, keepdims=True)
    )
    if state is not None:
        top = jnp.maximum(top, state[0])
    shift = top * SCALE
    expo = [jnp.exp2(s * SCALE - shift) for s in scores]
    total = jnp.sum(expo[0], axis=1, keepdims=True) + jnp.sum(expo[1], axis=1, keepdims=True)
    value = jnp.dot(expo[0].astype(jnp.bfloat16), blocks[0][:, QK:], preferred_element_type=jnp.float32)
    value = value + jnp.dot(
        expo[1].astype(jnp.bfloat16), blocks[1][:, QK:], preferred_element_type=jnp.float32
    )
    if state is not None:
        factor = jnp.exp2(state[0] * SCALE - shift)
        total = total + state[1] * factor
        value = value + state[2] * factor
    return top, total, value


def attend_first(q, own, sibling, top_out, total_out, value_out):
    for h in range(HEADS):
        top, total, value = attend(q, own, sibling, h, None)
        top_out[:, h : h + 1] = top
        total_out[:, h : h + 1] = total
        value_out[h] = value


def attend_second(q, own, sibling, top_in, total_in, value_in, heads):
    for h in range(HEADS):
        state = (top_in[:, h : h + 1], total_in[:, h : h + 1], value_in[h])
        top, total, value = attend(q, own, sibling, h, state)
        heads[:, h * VD : (h + 1) * VD] = (value / total).astype(jnp.bfloat16)


ATTEND_FLOPS = 2 * 192 * 8 * 1536 * 320


def output_kernel(spots, heads, pooled, a0, a1, b0, b1, mixed, columns, blocks, wide):
    for i in range(4):
        columns[i] = heads[:, i * 384 : i * 384 + 384]
    shards_dot(spots, 22, columns, ((a0, a1), (b0, b1)), blocks)
    for i in range(16):
        wide[:, i * 96 : i * 96 + 96] = blocks[i]
    mixed[...] = (pooled[...].astype(jnp.float32) + wide[...]).astype(jnp.bfloat16)


def output(spots, heads, pooled, own, sibling):
    return call(
        output_kernel,
        bf16(192, 1536),
        (
            pltpu.VMEM((4, 192, 384), jnp.bfloat16),
            pltpu.VMEM((16, 192, 96), jnp.float32),
            pltpu.VMEM((192, 1536), jnp.float32),
        ),
        2 * 192 * 1536 * 1536,
        "output",
        [smem()] + [vmem()] * 6,
    )(spots, heads, pooled, *own, *sibling)


def first(core):
    return 1 + 2 * core


def second(core):
    return 3 - 2 * core


def swap(value):
    return send(value, lambda x, y, z, c: (x, y, z, 1 - c))


def swapped(pairs):
    return swap(pairs[0]), swap(pairs[1])


def after(gate, *values):
    held = lax.optimization_barrier((*values, *gate))
    return held[0] if len(values) == 1 else held[: len(values)]


def to_first(value):
    return send(value, lambda x, y, z, c: (x ^ first(c), y, z, c))


def to_second(value):
    return send(value, lambda x, y, z, c: (x ^ second(c), y, z, c))


def to_far(value):
    return send(value, lambda x, y, z, c: (x ^ 2, y, z, c))


def across(value):
    return send(value, lambda x, y, z, c: (x, y, z + 4, c))


def x_pair(value):
    return jnp.stack([value, to_first(value)])


def x_four(pair):
    return jnp.concatenate([pair, to_second(pair)], axis=0)


def y_first(value):
    return jnp.stack([value, send(value, lambda x, y, z, c: (x, y ^ first(c), z, c))])


def y_second(pair):
    return pair, send(pair, lambda x, y, z, c: (x, y ^ second(c), z, c))


def z_step(z, c):
    return z ^ 1 if c == 0 else z + 2 * (z % 2) - 1


def z_first(value):
    return jnp.stack([value, send(value, lambda x, y, z, c: (x, y, z_step(z, c), c))])


def z_second(pair):
    return pair, send(pair, lambda x, y, z, c: (x, y, z_step(z, 1 - c), c))


def on_device(track, conv_weight, qkv_weight, out_weight):
    dp = lax.axis_index("dp")
    seq = lax.axis_index("seq")
    x, y, z_low, zh, core = (seq // 2) % 4, dp % 4, dp // 4, seq // 8, seq % 2
    spots = spots_of(x, y, z_low, zh, core)

    own = jnp.transpose(conv_weight, (1, 0, 2)).reshape(480, 1280)
    packed = pack(spots, own.reshape(4, 120, 1280), qkv_weight, out_weight)
    crossed = across(packed)
    near, beside = to_first(track), to_second(track)
    top = lax.ppermute(track[376:384], "seq", [(i, i + 1) for i in range(15)])
    bottom = lax.ppermute(track[0:8], "seq", [(i + 1, i) for i in range(15)])

    def unfold(rows):
        return jnp.concatenate([rows[:, i * 384 : i * 384 + 384] for i in range(3)], axis=0)

    def both(rows):
        pair = [unfold(packed[rows]), unfold(crossed[rows])]
        return jnp.where(zh == 0, jnp.stack(pair), jnp.stack(pair[::-1]))

    types = jnp.concatenate([both(slice(0, 32)), both(slice(32, 64))], axis=0)
    edges = x_four(x_pair(jnp.concatenate([top, bottom], axis=0)))
    sibling = swap(own)
    low = jnp.where(core == 0, own, sibling).reshape(5, 96, 1280)
    high = jnp.where(core == 0, sibling, own).reshape(5, 96, 1280)
    weight_a = jnp.concatenate([low, high], axis=1)
    act = gelu(track, edges[0])
    first_own = conv_a(act, weight_a)

    near, beside, types, edges, first_own, conv_crossed = after(
        (), near, beside, types, edges, first_own, crossed[64:184]
    )
    far = to_second(near)
    types = x_four(x_pair(types))
    others = y_second(y_first(conv_crossed))
    near, beside = gelu(near, edges[1]), gelu(beside, edges[2])
    first_near, first_beside = conv_a(near, weight_a), conv_a(beside, weight_a)

    far, types, *others = after((first_near, first_beside), far, types, *others)
    q_own, o_own = z_first(types[:, 0:2]), y_first(types[:, 2:4])
    weight_b = place(spots, others, swapped(others))

    tile_near = conv_b(near, weight_b, first_near)
    from_near = to_first(tile_near)
    q_own = z_second(after((tile_near,), q_own))
    tile_beside = conv_b(after((tile_near,), beside), weight_b, first_beside)
    from_beside = to_second(tile_beside)
    tile_own = conv_b(after((tile_beside,), act), weight_b, first_own)
    far, from_near, from_beside = after((tile_own,), far, from_near, from_beside)
    far = gelu(far, edges[3])
    tile_far = conv_b(far, weight_b, conv_a(far, weight_a))
    from_far = to_far(tile_far)
    tiles = [tile_own, from_near, from_beside, from_far]
    q_own = after((tile_far,), *q_own)
    q_sibling = swapped(q_own)
    o_own = y_second(after((tile_far,), o_own))

    pooled, columns, kv = key_value(spots, tiles, q_own, q_sibling)

    def spread(block):
        return [block, to_first(block), to_second(block), to_far(block)]

    *near_own, kv_cross, columns = after((), *spread(kv), across(kv), columns)
    near_own = jnp.stack(near_own)
    near_sibling = swap(near_own)
    queries = query(spots, columns, q_own, q_sibling)
    far_own = spread(kv_cross)
    state = call(
        attend_first, (f32(192, 8), f32(192, 8), f32(8, 192, 192)), flops=ATTEND_FLOPS, name="attend_first"
    )(queries, near_own, near_sibling)
    far_own = jnp.stack(after((state[0],), *far_own))
    far_sibling = swap(far_own)
    o_sibling = swap(after((queries,), o_own[0])), swap(after((far_sibling,), o_own[1]))
    heads = call(attend_second, bf16(192, 1536), flops=ATTEND_FLOPS, name="attend_second")(
        queries, far_own, far_sibling, *state
    )
    return output(spots, heads, pooled, o_own, o_sibling)


def solution(mesh):
    return jax.shard_map(
        on_device,
        mesh=mesh,
        in_specs=(P(("dp", "seq"), None), P("seq", None, None), P("seq", None), P("seq", None)),
        out_specs=P(("dp", "seq"), None),
        check_vma=False,
    )
```

```python
import functools

import jax
import jax.numpy as jnp
from jax import lax
from jax.experimental import pallas as pl
from jax.experimental.pallas import tpu as pltpu
from jax.sharding import PartitionSpec as P

HEADS = 8
QK = 128
VD = 192
EPS = 1e-06
AXES = ("dp", "seq")
MIB = 1024 * 1024
NT = (((1,), (1,)), ((), ()))


def spot(x, y, z, core):
    return ((z % 4) * 4 + y) * 16 + (z // 4) * 8 + x * 2 + core


def route(move):
    pairs = []
    for z in range(8):
        for y in range(4):
            for x in range(4):
                for core in range(2):
                    a, b, c, d = move(x, y, z, core)
                    pairs.append((spot(x, y, z, core), spot(a % 4, b % 4, c % 8, d % 2)))
    return pairs


def send(value, move):
    return lax.ppermute(value, AXES, route(move))


def call(body, out, scratch=(), flops=0, name=None, specs=None):
    extra = {} if specs is None else {"in_specs": specs}
    return pl.pallas_call(
        body,
        out_shape=out,
        scratch_shapes=list(scratch),
        compiler_params=pltpu.CompilerParams(vmem_limit_bytes=24 * MIB),
        cost_estimate=pl.CostEstimate(flops=0, bytes_accessed=0, transcendentals=0),
        name=name,
        **extra,
    )


def bf16(*shape):
    return jax.ShapeDtypeStruct(shape, jnp.bfloat16)


def f32(*shape):
    return jax.ShapeDtypeStruct(shape, jnp.float32)


def rms_scaled(values):
    return values * lax.rsqrt(jnp.mean(values * values, axis=-1, keepdims=True) + EPS)


def gelu_rows(values):
    return jax.nn.gelu(rms_scaled(values.astype(jnp.float32)))


def pack_kernel(spots, conv, qkv, out, packed):
    packed[0:64, 1152:1280] = jnp.zeros((64, 128), jnp.bfloat16)
    packed[0:32, 768:1152] = jnp.zeros((32, 384), jnp.bfloat16)
    for i in range(3):
        rows = min(32, 84 - 32 * i)
        packed[0:rows, i * 384 : i * 384 + 384] = qkv[32 * i : 32 * i + rows, :]
        packed[32:64, i * 384 : i * 384 + 384] = out[32 * i : 32 * i + 32, :]
    packed[64:184, :] = conv[0]


def pack(spots, conv, qkv, out):
    return pl.pallas_call(
        pack_kernel,
        grid_spec=pltpu.PrefetchScalarGridSpec(
            num_scalar_prefetch=1,
            grid=(1,),
            in_specs=[
                pl.BlockSpec((1, 120, 1280), lambda i, spots: (spots[22], 0, 0)),
                pl.BlockSpec((84, 384), lambda i, spots: (0, spots[14])),
                pl.BlockSpec((96, 384), lambda i, spots: (0, spots[22])),
            ],
            out_specs=pl.BlockSpec((184, 1280), lambda i, spots: (0, 0)),
        ),
        out_shape=bf16(184, 1280),
        name="pack",
    )(spots, conv, qkv, out)


def gelu_kernel(track, out):
    for i in range(0, 384, 48):
        out[i : i + 48, :] = gelu_rows(track[i : i + 48, :]).astype(jnp.bfloat16)


def gelu(track):
    return call(gelu_kernel, bf16(384, 1280), name="gelu")(track)


def shift_rows(place, act, edges, flat, shifted):
    edge = gelu_rows(edges[place]).astype(jnp.bfloat16).astype(jnp.float32)
    for c in range(10):
        cols = slice(c * 128, (c + 1) * 128)
        if act is not None:
            flat[c, 8:392, :] = act[:, cols].astype(jnp.float32)
        flat[c, 0:8, :] = edge[0:8, cols]
        flat[c, 392:400, :] = edge[8:16, cols]
        for j in range(6):
            shifted[j * 192 : (j + 1) * 192, cols] = flat[c, pl.ds(6 + j, 192, stride=2), :].astype(jnp.bfloat16)


def conv_tile(shifted, weight):
    total = jnp.zeros((384, 192), jnp.float32)
    for k in range(5):
        total = total + lax.dot_general(
            shifted[k * 192 : (k + 2) * 192, :], weight[k], NT, preferred_element_type=jnp.float32
        )
    return jnp.maximum(total[0:192], total[192:384]).astype(jnp.bfloat16)


def conv_first(place, act, edges, weight, out, flat, shifted):
    shift_rows(place, act, edges, flat, shifted)
    out[...] = conv_tile(shifted, weight)


def conv_second(place, act, edges, weight, first, out, flat, shifted):
    shift_rows(place, act, edges, flat, shifted)
    out[:, 0:192] = first[...]
    out[:, 192:384] = conv_tile(shifted, weight)


def spots_of(x, y, z_low, zh, core):
    def listed(v, c):
        one, three = v ^ 1, v ^ 3
        return [v, jnp.where(c == 0, one, three), jnp.where(c == 0, three, one), v ^ 2]

    def place(c):
        found = []
        for a in range(4):
            d = x ^ a
            near = jnp.where(d == 1, 1 + c, 2 - c)
            found.append(jnp.where(d == 0, 0, jnp.where(d == 2, 3, near)))
        return found

    values = [zh, core] + listed(x, core) + place(core) + place(1 - core)
    for v in (z_low, y):
        values += listed(v, core) + listed(v, 1 - core)
    return jnp.stack(values).astype(jnp.int32)


def conv_whole(track, edges, weight_a, weight_b, out, flat, shifted):
    for i in range(0, 384, 48):
        rows = gelu_rows(track[i : i + 48, :]).astype(jnp.bfloat16).astype(jnp.float32)
        for c in range(10):
            flat[c, 8 + i : 56 + i, :] = rows[:, c * 128 : (c + 1) * 128]
    shift_rows(3, None, edges, flat, shifted)
    out[:, 0:192] = conv_tile(shifted, weight_a)
    out[:, 192:384] = conv_tile(shifted, weight_b)


CONV_SCRATCH = (pltpu.VMEM((10, 400, 128), jnp.float32), pltpu.VMEM((1152, 1280), jnp.bfloat16))


def conv_a(place, act, edges, weight):
    body = functools.partial(conv_first, place)
    return call(body, bf16(192, 192), CONV_SCRATCH, 0, "conv_a")(act, edges, weight)


def conv_b(place, act, edges, weight, first):
    body = functools.partial(conv_second, place)
    return call(body, bf16(192, 384), CONV_SCRATCH, 0, "conv_b")(act, edges, weight, first)


def conv_far(track, edges, weight_a, weight_b):
    return call(conv_whole, bf16(192, 384), CONV_SCRATCH, 0, "conv_far")(track, edges, weight_a, weight_b)


def smem():
    return pl.BlockSpec(memory_space=pltpu.SMEM)


def vmem():
    return pl.BlockSpec(memory_space=pltpu.VMEM)


def place_kernel(spots, own0, own1, sib0, sib1, out, rows):
    core = spots[1]
    for side, pair in enumerate(((own0, own1), (sib0, sib1))):
        which = (core + side) % 2
        for r in range(4):
            quarter = spots[22 + 4 * side + r]
            rows[which * 4 + quarter] = pair[r // 2][r % 2]
    for c in range(2):
        whole = jnp.concatenate([rows[c * 4 + q] for q in range(4)], axis=0)
        for k in range(5):
            out[k, c * 96 : (c + 1) * 96, :] = whole[k * 96 : (k + 1) * 96]


def place(spots, own, sibling):
    return call(
        place_kernel,
        bf16(5, 192, 1280),
        (pltpu.VMEM((8, 120, 1280), jnp.bfloat16),),
        0,
        "place",
        [smem()] + [vmem()] * 4,
    )(spots, *own, *sibling)


def sort_kernel(spots, types, q, o):
    for t in range(8):
        place, zh = spots[6 + t % 4], t // 4
        q[t] = types[place, zh * 96 : zh * 96 + 96, :]
        o[t] = types[place, 192 + zh * 96 : 288 + zh * 96, :]


def sort(spots, types):
    return call(
        sort_kernel,
        (bf16(8, 96, 384), bf16(8, 96, 384)),
        name="sort",
        specs=[smem(), vmem()],
    )(spots, types)


def shards_dot(spots, base, columns, pairs, blocks):
    for side in range(2):
        count = pairs[side][0].shape[1]
        total = jnp.zeros((192, count * 96), jnp.float32)
        for r in range(4):
            weight = pairs[side][r // 2][r % 2].reshape(count * 96, 384)
            total = total + lax.dot_general(
                columns[spots[base + 4 * side + r]], weight, NT, preferred_element_type=jnp.float32
            )
        for t in range(count):
            blocks[2 * t + (spots[1] + side) % 2] = total[:, t * 96 : t * 96 + 96]


def key_value_kernel(spots, p0, p1, p2, p3, a0, a1, b0, b1, pooled, columns, kv, rest, tiles, blocks, wide):
    zh = spots[0]
    for s, piece in enumerate((p0, p1, p2, p3)):
        home = spots[2 + s]
        tiles[zh * 4 + home] = piece[:, 0:192]
        tiles[(1 - zh) * 4 + home] = piece[:, 192:384]
    for i in range(8):
        pooled[:, i * 192 : i * 192 + 192] = tiles[i]
    normed = rms_scaled(pooled[...].astype(jnp.float32)).astype(jnp.bfloat16)
    for i in range(4):
        columns[i] = normed[:, i * 384 : i * 384 + 384]
    shards_dot(spots, 14, columns, ((a0, a1), (b0, b1)), blocks)
    for i in range(4):
        wide[:, i * 84 : i * 84 + 84] = blocks[i][:, 0:84]
    kv[...] = wide[:, 16:336].astype(jnp.bfloat16)
    rest[...] = wide[:, 0:128].astype(jnp.bfloat16)


def key_value(spots, tiles, own, sibling):
    return call(
        key_value_kernel,
        (bf16(192, 1536), bf16(4, 192, 384), bf16(192, 320), bf16(192, 128)),
        (
            pltpu.VMEM((8, 192, 192), jnp.bfloat16),
            pltpu.VMEM((4, 192, 96), jnp.float32),
            pltpu.VMEM((192, 336), jnp.float32),
        ),
        name="key_value",
        specs=[smem()] + [vmem()] * 8,
    )(spots, *tiles, *own, *sibling)


def query_kernel(spots, columns, rest, a0, a1, b0, b1, q, blocks, wide):
    shards_dot(spots, 14, columns, ((a0, a1), (b0, b1)), blocks)
    for i in range(12):
        wide[:, i * 84 : i * 84 + 84] = blocks[i][:, 0:84]
    wide[:, 1008:1024] = rest[:, 0:16].astype(jnp.float32)
    q[...] = wide[...].astype(jnp.bfloat16)


def query(spots, columns, rest, own, sibling):
    return call(
        query_kernel,
        bf16(192, 1024),
        (pltpu.VMEM((12, 192, 96), jnp.float32), pltpu.VMEM((192, 1024), jnp.float32)),
        name="query",
        specs=[smem()] + [vmem()] * 6,
    )(spots, columns, rest, *own, *sibling)


SCALE = QK ** (-0.5) * 1.4426950408889634


def attend(q, own, sibling, h, state):
    query = q[:, h * QK : (h + 1) * QK]
    blocks = [own[...].reshape(768, 320), sibling[...].reshape(768, 320)]
    scores = [
        lax.dot_general(query, b[:, 0:QK], NT, preferred_element_type=jnp.float32) for b in blocks
    ]
    top = jnp.maximum(
        jnp.max(scores[0], axis=1, keepdims=True), jnp.max(scores[1], axis=1, keepdims=True)
    )
    if state is not None:
        top = jnp.maximum(top, state[0])
    shift = top * SCALE
    expo = [jnp.exp2(s * SCALE - shift) for s in scores]
    total = jnp.sum(expo[0], axis=1, keepdims=True) + jnp.sum(expo[1], axis=1, keepdims=True)
    value = jnp.dot(expo[0].astype(jnp.bfloat16), blocks[0][:, QK:], preferred_element_type=jnp.float32)
    value = value + jnp.dot(
        expo[1].astype(jnp.bfloat16), blocks[1][:, QK:], preferred_element_type=jnp.float32
    )
    if state is not None:
        factor = jnp.exp2(state[0] * SCALE - shift)
        total = total + state[1] * factor
        value = value + state[2] * factor
    return top, total, value


def attend_first(q, own, sibling, top_out, total_out, value_out):
    for h in range(HEADS):
        top, total, value = attend(q, own, sibling, h, None)
        top_out[:, h : h + 1] = top
        total_out[:, h : h + 1] = total
        value_out[h] = value


def attend_second(q, own, sibling, top_in, total_in, value_in, heads):
    for h in range(HEADS):
        state = (top_in[:, h : h + 1], total_in[:, h : h + 1], value_in[h])
        top, total, value = attend(q, own, sibling, h, state)
        heads[:, h * VD : (h + 1) * VD] = (value / total).astype(jnp.bfloat16)


def output_kernel(spots, heads, pooled, a0, a1, b0, b1, mixed, columns, blocks, wide):
    for i in range(4):
        columns[i] = heads[:, i * 384 : i * 384 + 384]
    shards_dot(spots, 22, columns, ((a0, a1), (b0, b1)), blocks)
    for i in range(16):
        wide[:, i * 96 : i * 96 + 96] = blocks[i]
    mixed[...] = (pooled[...].astype(jnp.float32) + wide[...]).astype(jnp.bfloat16)


def output(spots, heads, pooled, own, sibling):
    return call(
        output_kernel,
        bf16(192, 1536),
        (
            pltpu.VMEM((4, 192, 384), jnp.bfloat16),
            pltpu.VMEM((16, 192, 96), jnp.float32),
            pltpu.VMEM((192, 1536), jnp.float32),
        ),
        2 * 192 * 1536 * 1536,
        "output",
        [smem()] + [vmem()] * 6,
    )(spots, heads, pooled, *own, *sibling)


def first(core):
    return 1 + 2 * core


def second(core):
    return 3 - 2 * core


def swap(value):
    return send(value, lambda x, y, z, c: (x, y, z, 1 - c))


def swapped(pairs):
    return swap(pairs[0]), swap(pairs[1])


def after(gate, *values):
    held = lax.optimization_barrier((*values, *gate))
    return held[0] if len(values) == 1 else held[: len(values)]


def to_first(value):
    return send(value, lambda x, y, z, c: (x ^ first(c), y, z, c))


def to_second(value):
    return send(value, lambda x, y, z, c: (x ^ second(c), y, z, c))


def to_far(value):
    return send(value, lambda x, y, z, c: (x ^ 2, y, z, c))


def across(value):
    return send(value, lambda x, y, z, c: (x, y, z + 4, c))


def x_pair(value):
    return jnp.stack([value, to_first(value)])


def x_four(pair):
    return jnp.concatenate([pair, to_second(pair)], axis=0)


def y_first(value):
    return value, send(value, lambda x, y, z, c: (x, y ^ first(c), z, c))


def y_second(pair):
    return pair, send(pair, lambda x, y, z, c: (x, y ^ second(c), z, c))


def z_step(z, c):
    return z ^ 1 if c == 0 else z + 2 * (z % 2) - 1


def z_first(value):
    return value, send(value, lambda x, y, z, c: (x, y, z_step(z, c), c))


def z_second(pair):
    return pair, send(pair, lambda x, y, z, c: (x, y, z_step(z, 1 - c), c))


def on_device(track, conv_weight, qkv_weight, out_weight):
    dp = lax.axis_index("dp")
    seq = lax.axis_index("seq")
    x, y, z_low, zh, core = (seq // 2) % 4, dp % 4, dp // 4, seq // 8, seq % 2
    spots = spots_of(x, y, z_low, zh, core)

    own = jnp.transpose(conv_weight, (1, 0, 2)).reshape(480, 1280)
    packed = pack(spots, own.reshape(4, 120, 1280), qkv_weight, out_weight)
    top = lax.ppermute(track[376:384], "seq", [(i, i + 1) for i in range(15)])
    bottom = lax.ppermute(track[0:8], "seq", [(i + 1, i) for i in range(15)])
    crossed = across(packed)
    near, beside = to_first(track), to_second(track)

    def unfold(rows):
        return jnp.concatenate([rows[:, i * 384 : i * 384 + 384] for i in range(3)], axis=0)

    def both(rows):
        pair = [unfold(packed[rows]), unfold(crossed[rows])]
        return jnp.where(zh == 0, jnp.stack(pair), jnp.stack(pair[::-1]))

    types = [both(rows).reshape(192, 384) for rows in (slice(0, 32), slice(32, 64))]
    sibling = swap(own)
    low = jnp.where(core == 0, own, sibling).reshape(5, 96, 1280)
    high = jnp.where(core == 0, sibling, own).reshape(5, 96, 1280)
    weight_a = jnp.concatenate([low, high], axis=1)

    near, beside, top, bottom, conv_crossed, *types = after(
        (), near, beside, top, bottom, crossed[64:184], *types
    )
    edges = x_pair(jnp.concatenate([top, bottom], axis=0))
    all_edges = x_four(edges)
    types = x_four(x_pair(jnp.concatenate(types, axis=0)))
    far = to_second(near)
    others = jnp.stack(y_first(conv_crossed))
    others_sibling = swap(others)
    others_far = y_second(others)[1]

    q_types, o_types = sort(spots, types)
    q_near = z_first(q_types)[1]
    act, near, beside = gelu(track), gelu(near), gelu(beside)
    first_own, first_near, first_beside = [
        conv_a(i, block, some, weight_a)
        for i, (block, some) in enumerate(((act, edges), (near, edges), (beside, all_edges)))
    ]
    weight_b = place(spots, (others, others_far), (others_sibling, swap(others_far)))
    weight_b = after((first_own, first_near, first_beside), weight_b)
    o_own = y_first(o_types)

    tile_near = conv_b(1, near, edges, weight_b, first_near)
    from_near = to_first(tile_near)
    far, q_near = after((tile_near,), far, q_near)
    kv_own = z_second(jnp.stack([q_types[6:8], q_near[6:8]]))
    tile_far = conv_far(far, all_edges, weight_a, weight_b)
    from_far = to_far(tile_far)
    tile_beside = conv_b(2, after((tile_far,), beside), all_edges, weight_b, first_beside)
    from_beside = to_second(tile_beside)
    gate = (tile_beside, from_near, from_far, *kv_own)
    act, q_types, q_near, *kv_own = after(gate, act, q_types, q_near, *kv_own)
    kv_sibling = swapped(kv_own)
    q_own = z_second(jnp.stack([q_types[0:6], q_near[0:6]]))
    tile_own = conv_b(0, act, edges, weight_b, first_own)
    tiles = [tile_own, from_near, from_beside, from_far]

    pooled, columns, kv, rest = key_value(spots, tiles, kv_own, kv_sibling)

    def spread(block):
        return [block, to_first(block), to_second(block), to_far(block)]

    q_far = after((kv,), q_own[1])
    o_own = y_second(jnp.stack(after((kv,), *o_own)))
    q_own, q_sibling = (q_own[0], q_far), (swap(after((tile_far,), q_own[0])), swap(q_far))
    queries = query(spots, columns, rest, q_own, q_sibling)
    kv_cross, *near_own, queries, o_far = after((), across(kv), *spread(kv), queries, o_own[1])
    near_own = jnp.stack(near_own)
    near_sibling = swap(near_own)
    far_own = spread(kv_cross)
    state = call(
        attend_first, (f32(192, 8), f32(192, 8), f32(8, 192, 192)), name="attend_first"
    )(queries, near_own, near_sibling)
    far_own = jnp.stack(after((state[0],), *far_own))
    far_sibling = swap(far_own)
    o_own = o_own[0], o_far
    o_sibling = swapped(after((queries,), *o_own))
    heads = call(attend_second, bf16(192, 1536), name="attend_second")(
        queries, far_own, far_sibling, *state
    )
    return output(spots, heads, pooled, o_own, o_sibling)


def solution(mesh):
    return jax.shard_map(
        on_device,
        mesh=mesh,
        in_specs=(P(("dp", "seq"), None), P("seq", None, None), P("seq", None), P("seq", None)),
        out_specs=P(("dp", "seq"), None),
        check_vma=False,
    )
```

```python
import functools

import jax
import jax.numpy as jnp
from jax import lax
from jax.experimental import pallas as pl
from jax.experimental.pallas import tpu as pltpu
from jax.sharding import PartitionSpec as P

HEADS = 8
QK = 128
VD = 192
EPS = 1e-06
AXES = ("dp", "seq")
MIB = 1024 * 1024
NT = (((1,), (1,)), ((), ()))


def spot(x, y, z, core):
    return ((z % 4) * 4 + y) * 16 + (z // 4) * 8 + x * 2 + core


def route(move):
    pairs = []
    for z in range(8):
        for y in range(4):
            for x in range(4):
                for core in range(2):
                    a, b, c, d = move(x, y, z, core)
                    pairs.append((spot(x, y, z, core), spot(a % 4, b % 4, c % 8, d % 2)))
    return pairs


def send(value, move):
    return lax.ppermute(value, AXES, route(move))


def call(body, out, scratch=(), flops=0, name=None, specs=None):
    extra = {} if specs is None else {"in_specs": specs}
    return pl.pallas_call(
        body,
        out_shape=out,
        scratch_shapes=list(scratch),
        compiler_params=pltpu.CompilerParams(vmem_limit_bytes=24 * MIB),
        cost_estimate=pl.CostEstimate(flops=0, bytes_accessed=0, transcendentals=0),
        name=name,
        **extra,
    )


def bf16(*shape):
    return jax.ShapeDtypeStruct(shape, jnp.bfloat16)


def f32(*shape):
    return jax.ShapeDtypeStruct(shape, jnp.float32)


def rms_scaled(values):
    return values * lax.rsqrt(jnp.mean(values * values, axis=-1, keepdims=True) + EPS)


def gelu_rows(values):
    return jax.nn.gelu(rms_scaled(values.astype(jnp.float32)))


def pack_kernel(spots, conv, qkv, out, packed):
    packed[0:64, 1152:1280] = jnp.zeros((64, 128), jnp.bfloat16)
    packed[0:32, 768:1152] = jnp.zeros((32, 384), jnp.bfloat16)
    for i in range(3):
        rows = min(32, 84 - 32 * i)
        packed[0:rows, i * 384 : i * 384 + 384] = qkv[32 * i : 32 * i + rows, :]
        packed[32:64, i * 384 : i * 384 + 384] = out[32 * i : 32 * i + 32, :]
    packed[64:184, :] = conv[0]


def pack(spots, conv, qkv, out):
    return pl.pallas_call(
        pack_kernel,
        grid_spec=pltpu.PrefetchScalarGridSpec(
            num_scalar_prefetch=1,
            grid=(1,),
            in_specs=[
                pl.BlockSpec((1, 120, 1280), lambda i, spots: (spots[22], 0, 0)),
                pl.BlockSpec((84, 384), lambda i, spots: (0, spots[14])),
                pl.BlockSpec((96, 384), lambda i, spots: (0, spots[22])),
            ],
            out_specs=pl.BlockSpec((184, 1280), lambda i, spots: (0, 0)),
        ),
        out_shape=bf16(184, 1280),
        name="pack",
    )(spots, conv, qkv, out)


def gelu_kernel(track, out):
    for i in range(0, 384, 48):
        out[i : i + 48, :] = gelu_rows(track[i : i + 48, :]).astype(jnp.bfloat16)


def gelu(track):
    return call(gelu_kernel, bf16(384, 1280), name="gelu")(track)


def shift_rows(place, act, edges, flat, shifted):
    edge = gelu_rows(edges[place]).astype(jnp.bfloat16).astype(jnp.float32)
    for c in range(10):
        cols = slice(c * 128, (c + 1) * 128)
        if act is not None:
            flat[c, 8:392, :] = act[:, cols].astype(jnp.float32)
        flat[c, 0:8, :] = edge[0:8, cols]
        flat[c, 392:400, :] = edge[8:16, cols]
        for j in range(6):
            shifted[j * 192 : (j + 1) * 192, cols] = flat[c, pl.ds(6 + j, 192, stride=2), :].astype(jnp.bfloat16)


def conv_tile(shifted, weight):
    total = jnp.zeros((384, 192), jnp.float32)
    for k in range(5):
        total = total + lax.dot_general(
            shifted[k * 192 : (k + 2) * 192, :], weight[k], NT, preferred_element_type=jnp.float32
        )
    return jnp.maximum(total[0:192], total[192:384]).astype(jnp.bfloat16)


def conv_first(place, act, edges, weight, out, flat, shifted):
    shift_rows(place, act, edges, flat, shifted)
    out[...] = conv_tile(shifted, weight)


def conv_second(place, act, edges, weight, first, out, flat, shifted):
    shift_rows(place, act, edges, flat, shifted)
    out[:, 0:192] = first[...]
    out[:, 192:384] = conv_tile(shifted, weight)


def spots_of(x, y, z_low, zh, core):
    def listed(v, c):
        one, three = v ^ 1, v ^ 3
        return [v, jnp.where(c == 0, one, three), jnp.where(c == 0, three, one), v ^ 2]

    def place(c):
        found = []
        for a in range(4):
            d = x ^ a
            near = jnp.where(d == 1, 1 + c, 2 - c)
            found.append(jnp.where(d == 0, 0, jnp.where(d == 2, 3, near)))
        return found

    values = [zh, core] + listed(x, core) + place(core) + place(1 - core)
    for v in (z_low, y):
        values += listed(v, core) + listed(v, 1 - core)
    return jnp.stack(values).astype(jnp.int32)


def conv_whole(track, edges, weight_a, weight_b, out, flat, shifted):
    for i in range(0, 384, 48):
        rows = gelu_rows(track[i : i + 48, :]).astype(jnp.bfloat16).astype(jnp.float32)
        for c in range(10):
            flat[c, 8 + i : 56 + i, :] = rows[:, c * 128 : (c + 1) * 128]
    shift_rows(3, None, edges, flat, shifted)
    out[:, 0:192] = conv_tile(shifted, weight_a)
    out[:, 192:384] = conv_tile(shifted, weight_b)


CONV_SCRATCH = (pltpu.VMEM((10, 400, 128), jnp.float32), pltpu.VMEM((1152, 1280), jnp.bfloat16))


def conv_a(place, act, edges, weight):
    body = functools.partial(conv_first, place)
    return call(body, bf16(192, 192), CONV_SCRATCH, 0, "conv_a")(act, edges, weight)


def conv_b(place, act, edges, weight, first):
    body = functools.partial(conv_second, place)
    return call(body, bf16(192, 384), CONV_SCRATCH, 0, "conv_b")(act, edges, weight, first)


def conv_far(track, edges, weight_a, weight_b):
    return call(conv_whole, bf16(192, 384), CONV_SCRATCH, 0, "conv_far")(track, edges, weight_a, weight_b)


def smem():
    return pl.BlockSpec(memory_space=pltpu.SMEM)


def vmem():
    return pl.BlockSpec(memory_space=pltpu.VMEM)


def place_kernel(spots, own0, own1, sib0, sib1, out, rows):
    core = spots[1]
    for side, pair in enumerate(((own0, own1), (sib0, sib1))):
        which = (core + side) % 2
        for r in range(4):
            quarter = spots[22 + 4 * side + r]
            rows[which * 4 + quarter] = pair[r // 2][r % 2]
    for c in range(2):
        whole = jnp.concatenate([rows[c * 4 + q] for q in range(4)], axis=0)
        for k in range(5):
            out[k, c * 96 : (c + 1) * 96, :] = whole[k * 96 : (k + 1) * 96]


def place(spots, own, sibling):
    return call(
        place_kernel,
        bf16(5, 192, 1280),
        (pltpu.VMEM((8, 120, 1280), jnp.bfloat16),),
        0,
        "place",
        [smem()] + [vmem()] * 4,
    )(spots, *own, *sibling)


def sort_kernel(spots, types, q, o):
    for t in range(8):
        place, zh = spots[6 + t % 4], t // 4
        q[t] = types[place, zh * 96 : zh * 96 + 96, :]
        o[t] = types[place, 192 + zh * 96 : 288 + zh * 96, :]


def sort(spots, types):
    return call(
        sort_kernel,
        (bf16(8, 96, 384), bf16(8, 96, 384)),
        name="sort",
        specs=[smem(), vmem()],
    )(spots, types)


def shards_dot(spots, base, columns, pairs, blocks):
    for side in range(2):
        count = pairs[side][0].shape[1]
        total = jnp.zeros((192, count * 96), jnp.float32)
        for r in range(4):
            weight = pairs[side][r // 2][r % 2].reshape(count * 96, 384)
            total = total + lax.dot_general(
                columns[spots[base + 4 * side + r]], weight, NT, preferred_element_type=jnp.float32
            )
        for t in range(count):
            blocks[2 * t + (spots[1] + side) % 2] = total[:, t * 96 : t * 96 + 96]


def key_value_kernel(spots, p0, p1, p2, p3, a0, a1, b0, b1, pooled, columns, kv, rest, tiles, blocks, wide):
    zh = spots[0]
    for s, piece in enumerate((p0, p1, p2, p3)):
        home = spots[2 + s]
        tiles[zh * 4 + home] = piece[:, 0:192]
        tiles[(1 - zh) * 4 + home] = piece[:, 192:384]
    for i in range(8):
        pooled[:, i * 192 : i * 192 + 192] = tiles[i]
    normed = rms_scaled(pooled[...].astype(jnp.float32)).astype(jnp.bfloat16)
    for i in range(4):
        columns[i] = normed[:, i * 384 : i * 384 + 384]
    shards_dot(spots, 14, columns, ((a0, a1), (b0, b1)), blocks)
    for i in range(4):
        wide[:, i * 84 : i * 84 + 84] = blocks[i][:, 0:84]
    kv[...] = wide[:, 16:336].astype(jnp.bfloat16)
    rest[...] = wide[:, 0:128].astype(jnp.bfloat16)


def key_value(spots, tiles, own, sibling):
    return call(
        key_value_kernel,
        (bf16(192, 1536), bf16(4, 192, 384), bf16(192, 320), bf16(192, 128)),
        (
            pltpu.VMEM((8, 192, 192), jnp.bfloat16),
            pltpu.VMEM((4, 192, 96), jnp.float32),
            pltpu.VMEM((192, 336), jnp.float32),
        ),
        name="key_value",
        specs=[smem()] + [vmem()] * 8,
    )(spots, *tiles, *own, *sibling)


def shards_columns(spots, base, columns, pairs, blocks):
    for side in range(2):
        count = pairs[side][0].shape[1]
        total = jnp.zeros((count * 96, 192), jnp.float32)
        for r in range(4):
            weight = pairs[side][r // 2][r % 2].reshape(count * 96, 384)
            total = total + lax.dot_general(
                weight, columns[spots[base + 4 * side + r]], NT, preferred_element_type=jnp.float32
            )
        for t in range(count):
            blocks[2 * t + (spots[1] + side) % 2] = total[t * 96 : t * 96 + 96, :]


def query_kernel(spots, columns, rest, a0, a1, b0, b1, q, blocks, wide):
    shards_columns(spots, 14, columns, ((a0, a1), (b0, b1)), blocks)
    for i in range(12):
        wide[i * 84 : i * 84 + 84, :] = blocks[i, 0:84]
    q[:, 0:896] = jnp.transpose(wide[0:896, :]).astype(jnp.bfloat16)
    last = jnp.concatenate([jnp.transpose(wide[896:1024, :])[:, 0:112], rest[:, 0:16].astype(jnp.float32)], axis=1)
    q[:, 896:1024] = last.astype(jnp.bfloat16)


def query(spots, columns, rest, own, sibling):
    return call(
        query_kernel,
        bf16(192, 1024),
        (pltpu.VMEM((12, 96, 192), jnp.float32), pltpu.VMEM((1024, 192), jnp.float32)),
        name="query",
        specs=[smem()] + [vmem()] * 6,
    )(spots, columns, rest, *own, *sibling)


SCALE = QK ** (-0.5) * 1.4426950408889634


def attend(q, own, sibling, h, state):
    query = q[:, h * QK : (h + 1) * QK]
    blocks = [own[...].reshape(768, 320), sibling[...].reshape(768, 320)]
    scores = [
        lax.dot_general(query, b[:, 0:QK], NT, preferred_element_type=jnp.float32) for b in blocks
    ]
    top = jnp.maximum(
        jnp.max(scores[0], axis=1, keepdims=True), jnp.max(scores[1], axis=1, keepdims=True)
    )
    if state is not None:
        top = jnp.maximum(top, state[0])
    shift = top * SCALE
    expo = [jnp.exp2(s * SCALE - shift) for s in scores]
    total = jnp.sum(expo[0], axis=1, keepdims=True) + jnp.sum(expo[1], axis=1, keepdims=True)
    value = jnp.dot(expo[0].astype(jnp.bfloat16), blocks[0][:, QK:], preferred_element_type=jnp.float32)
    value = value + jnp.dot(
        expo[1].astype(jnp.bfloat16), blocks[1][:, QK:], preferred_element_type=jnp.float32
    )
    if state is not None:
        factor = jnp.exp2(state[0] * SCALE - shift)
        total = total + state[1] * factor
        value = value + state[2] * factor
    return top, total, value


def attend_first(q, own, sibling, top_out, total_out, value_out):
    for h in range(HEADS):
        top, total, value = attend(q, own, sibling, h, None)
        top_out[:, h : h + 1] = top
        total_out[:, h : h + 1] = total
        value_out[h] = value


def attend_second(q, own, sibling, top_in, total_in, value_in, heads):
    for h in range(HEADS):
        state = (top_in[:, h : h + 1], total_in[:, h : h + 1], value_in[h])
        top, total, value = attend(q, own, sibling, h, state)
        heads[:, h * VD : (h + 1) * VD] = (value / total).astype(jnp.bfloat16)


def output_kernel(spots, heads, pooled, a0, a1, b0, b1, mixed, columns, blocks):
    for i in range(4):
        columns[i] = heads[:, i * 384 : i * 384 + 384]
    shards_columns(spots, 22, columns, ((a0, a1), (b0, b1)), blocks)
    for i in range(4):
        cols = slice(i * 384, i * 384 + 384)
        part = jnp.transpose(blocks[i * 4 : i * 4 + 4].reshape(384, 192))
        mixed[:, cols] = (pooled[:, cols].astype(jnp.float32) + part).astype(jnp.bfloat16)


def output(spots, heads, pooled, own, sibling):
    return call(
        output_kernel,
        bf16(192, 1536),
        (
            pltpu.VMEM((4, 192, 384), jnp.bfloat16),
            pltpu.VMEM((16, 96, 192), jnp.float32),
        ),
        2 * 192 * 1536 * 1536,
        "output",
        [smem()] + [vmem()] * 6,
    )(spots, heads, pooled, *own, *sibling)


def first(core):
    return 1 + 2 * core


def second(core):
    return 3 - 2 * core


def swap(value):
    return send(value, lambda x, y, z, c: (x, y, z, 1 - c))


def swapped(pairs):
    return swap(pairs[0]), swap(pairs[1])


def after(gate, *values):
    held = lax.optimization_barrier((*values, *gate))
    return held[0] if len(values) == 1 else held[: len(values)]


def to_first(value):
    return send(value, lambda x, y, z, c: (x ^ first(c), y, z, c))


def to_second(value):
    return send(value, lambda x, y, z, c: (x ^ second(c), y, z, c))


def to_far(value):
    return send(value, lambda x, y, z, c: (x ^ 2, y, z, c))


def across(value):
    return send(value, lambda x, y, z, c: (x, y, z + 4, c))


def x_pair(value):
    return jnp.stack([value, to_first(value)])


def x_four(pair):
    return jnp.concatenate([pair, to_second(pair)], axis=0)


def y_first(value):
    return value, send(value, lambda x, y, z, c: (x, y ^ first(c), z, c))


def y_second(pair):
    return pair, send(pair, lambda x, y, z, c: (x, y ^ second(c), z, c))


def z_step(z, c):
    return z ^ 1 if c == 0 else z + 2 * (z % 2) - 1


def z_first(value):
    return value, send(value, lambda x, y, z, c: (x, y, z_step(z, c), c))


def z_second(pair):
    return pair, send(pair, lambda x, y, z, c: (x, y, z_step(z, 1 - c), c))


def on_device(track, conv_weight, qkv_weight, out_weight):
    dp = lax.axis_index("dp")
    seq = lax.axis_index("seq")
    x, y, z_low, zh, core = (seq // 2) % 4, dp % 4, dp // 4, seq // 8, seq % 2
    spots = spots_of(x, y, z_low, zh, core)

    own = jnp.transpose(conv_weight, (1, 0, 2)).reshape(480, 1280)
    packed = pack(spots, own.reshape(4, 120, 1280), qkv_weight, out_weight)
    top = lax.ppermute(track[376:384], "seq", [(i, i + 1) for i in range(15)])
    bottom = lax.ppermute(track[0:8], "seq", [(i + 1, i) for i in range(15)])
    crossed = across(packed)
    near, beside = to_first(track), to_second(track)

    def unfold(rows):
        return jnp.concatenate([rows[:, i * 384 : i * 384 + 384] for i in range(3)], axis=0)

    def both(rows):
        pair = [unfold(packed[rows]), unfold(crossed[rows])]
        return jnp.where(zh == 0, jnp.stack(pair), jnp.stack(pair[::-1]))

    types = [both(rows).reshape(192, 384) for rows in (slice(0, 32), slice(32, 64))]
    sibling = swap(own)
    low = jnp.where(core == 0, own, sibling).reshape(5, 96, 1280)
    high = jnp.where(core == 0, sibling, own).reshape(5, 96, 1280)
    weight_a = jnp.concatenate([low, high], axis=1)

    near, beside, top, bottom, conv_crossed, *types = after(
        (), near, beside, top, bottom, crossed[64:184], *types
    )
    edges = x_pair(jnp.concatenate([top, bottom], axis=0))
    all_edges = x_four(edges)
    types = x_four(x_pair(jnp.concatenate(types, axis=0)))
    far = to_second(near)
    others = jnp.stack(y_first(conv_crossed))
    others_sibling = swap(others)
    others_far = y_second(others)[1]

    q_types, o_types = sort(spots, types)
    q_near = z_first(q_types)[1]
    act, near, beside = gelu(track), gelu(near), gelu(beside)
    first_own, first_near = conv_a(0, act, edges, weight_a), conv_a(1, near, edges, weight_a)
    all_edges = after((first_own, first_near), all_edges)
    first_beside = conv_a(2, beside, all_edges, weight_a)
    weight_b = place(spots, (others, others_far), (others_sibling, swap(others_far)))
    weight_b = after((first_own, first_near, first_beside), weight_b)
    o_own = y_first(o_types)

    tile_near = conv_b(1, near, edges, weight_b, first_near)
    from_near = to_first(tile_near)
    far, q_near = after((tile_near,), far, q_near)
    kv_own = z_second(jnp.stack([q_types[6:8], q_near[6:8]]))
    tile_far = conv_far(far, all_edges, weight_a, weight_b)
    from_far = to_far(tile_far)
    tile_beside = conv_b(2, after((tile_far,), beside), all_edges, weight_b, first_beside)
    from_beside = to_second(tile_beside)
    gate = (tile_beside, from_near, from_far, *kv_own)
    act, q_types, q_near, *kv_own = after(gate, act, q_types, q_near, *kv_own)
    kv_sibling = swapped(kv_own)
    q_own = z_second(jnp.stack([q_types[0:6], q_near[0:6]]))
    tile_own = conv_b(0, act, edges, weight_b, first_own)
    tiles = [tile_own, from_near, from_beside, from_far]

    pooled, columns, kv, rest = key_value(spots, tiles, kv_own, kv_sibling)

    def spread(block):
        return [block, to_first(block), to_second(block), to_far(block)]

    q_far = after((kv,), q_own[1])
    o_own = y_second(jnp.stack(after((kv,), *o_own)))
    q_own, q_sibling = (q_own[0], q_far), (swap(after((tile_far,), q_own[0])), swap(q_far))
    queries = query(spots, columns, rest, q_own, q_sibling)
    kv_cross, *near_own, queries, o_far = after((), across(kv), *spread(kv), queries, o_own[1])
    near_own = jnp.stack(near_own)
    near_sibling = swap(near_own)
    far_own = spread(kv_cross)
    state = call(
        attend_first, (f32(192, 8), f32(192, 8), f32(8, 192, 192)), name="attend_first"
    )(queries, near_own, near_sibling)
    far_own = jnp.stack(after((state[0],), *far_own))
    far_sibling = swap(far_own)
    o_own = o_own[0], o_far
    o_sibling = swapped(after((queries,), *o_own))
    heads = call(attend_second, bf16(192, 1536), name="attend_second")(
        queries, far_own, far_sibling, *state
    )
    return output(spots, heads, pooled, o_own, o_sibling)


def solution(mesh):
    return jax.shard_map(
        on_device,
        mesh=mesh,
        in_specs=(P(("dp", "seq"), None), P("seq", None, None), P("seq", None), P("seq", None)),
        out_specs=P(("dp", "seq"), None),
        check_vma=False,
    )
```

```python
import functools

import jax
import jax.numpy as jnp
from jax import lax
from jax.experimental import pallas as pl
from jax.experimental.pallas import tpu as pltpu
from jax.sharding import PartitionSpec as P

HEADS = 8
QK = 128
VD = 192
EPS = 1e-06
AXES = ("dp", "seq")
MIB = 1024 * 1024
NT = (((1,), (1,)), ((), ()))


def spot(x, y, z, core):
    return ((z % 4) * 4 + y) * 16 + (z // 4) * 8 + x * 2 + core


def route(move):
    pairs = []
    for z in range(8):
        for y in range(4):
            for x in range(4):
                for core in range(2):
                    a, b, c, d = move(x, y, z, core)
                    pairs.append((spot(x, y, z, core), spot(a % 4, b % 4, c % 8, d % 2)))
    return pairs


def send(value, move):
    return lax.ppermute(value, AXES, route(move))


def call(body, out, scratch=(), flops=0, name=None, specs=None):
    extra = {} if specs is None else {"in_specs": specs}
    return pl.pallas_call(
        body,
        out_shape=out,
        scratch_shapes=list(scratch),
        compiler_params=pltpu.CompilerParams(vmem_limit_bytes=24 * MIB),
        cost_estimate=pl.CostEstimate(flops=0, bytes_accessed=0, transcendentals=0),
        name=name,
        **extra,
    )


def bf16(*shape):
    return jax.ShapeDtypeStruct(shape, jnp.bfloat16)


def f32(*shape):
    return jax.ShapeDtypeStruct(shape, jnp.float32)


def rms_scaled(values):
    return values * lax.rsqrt(jnp.mean(values * values, axis=-1, keepdims=True) + EPS)


def gelu_rows(values):
    return jax.nn.gelu(rms_scaled(values.astype(jnp.float32)))


def pack_kernel(spots, conv, qkv, out, packed):
    packed[0:64, 1152:1280] = jnp.zeros((64, 128), jnp.bfloat16)
    packed[0:32, 768:1152] = jnp.zeros((32, 384), jnp.bfloat16)
    for i in range(3):
        rows = min(32, 84 - 32 * i)
        packed[0:rows, i * 384 : i * 384 + 384] = qkv[32 * i : 32 * i + rows, :]
        packed[32:64, i * 384 : i * 384 + 384] = out[32 * i : 32 * i + 32, :]
    packed[64:184, :] = conv[0]


def pack(spots, conv, qkv, out):
    return pl.pallas_call(
        pack_kernel,
        grid_spec=pltpu.PrefetchScalarGridSpec(
            num_scalar_prefetch=1,
            grid=(1,),
            in_specs=[
                pl.BlockSpec((1, 120, 1280), lambda i, spots: (spots[22], 0, 0)),
                pl.BlockSpec((84, 384), lambda i, spots: (0, spots[14])),
                pl.BlockSpec((96, 384), lambda i, spots: (0, spots[22])),
            ],
            out_specs=pl.BlockSpec((184, 1280), lambda i, spots: (0, 0)),
        ),
        out_shape=bf16(184, 1280),
        name="pack",
    )(spots, conv, qkv, out)


def gelu_kernel(track, out):
    for i in range(0, 384, 48):
        out[i : i + 48, :] = gelu_rows(track[i : i + 48, :]).astype(jnp.bfloat16)


def gelu(track):
    return call(gelu_kernel, bf16(384, 1280), name="gelu")(track)


def shift_rows(place, act, edges, flat, shifted):
    edge = gelu_rows(edges[place]).astype(jnp.bfloat16).astype(jnp.float32)
    for c in range(10):
        cols = slice(c * 128, (c + 1) * 128)
        if act is not None:
            flat[c, 8:392, :] = act[:, cols].astype(jnp.float32)
        flat[c, 0:8, :] = edge[0:8, cols]
        flat[c, 392:400, :] = edge[8:16, cols]
        for j in range(6):
            shifted[j * 192 : (j + 1) * 192, cols] = flat[c, pl.ds(6 + j, 192, stride=2), :].astype(jnp.bfloat16)


def conv_tile(shifted, weight):
    total = jnp.zeros((384, 192), jnp.float32)
    for k in range(5):
        total = total + lax.dot_general(
            shifted[k * 192 : (k + 2) * 192, :], weight[k], NT, preferred_element_type=jnp.float32
        )
    return jnp.maximum(total[0:192], total[192:384]).astype(jnp.bfloat16)


def conv_first(place, act, edges, weight, out, flat, shifted):
    shift_rows(place, act, edges, flat, shifted)
    out[...] = conv_tile(shifted, weight)


def conv_second(place, act, edges, weight, first, out, flat, shifted):
    shift_rows(place, act, edges, flat, shifted)
    out[:, 0:192] = first[...]
    out[:, 192:384] = conv_tile(shifted, weight)


def spots_of(x, y, z_low, zh, core):
    def listed(v, c):
        one, three = v ^ 1, v ^ 3
        return [v, jnp.where(c == 0, one, three), jnp.where(c == 0, three, one), v ^ 2]

    def place(c):
        found = []
        for a in range(4):
            d = x ^ a
            near = jnp.where(d == 1, 1 + c, 2 - c)
            found.append(jnp.where(d == 0, 0, jnp.where(d == 2, 3, near)))
        return found

    values = [zh, core] + listed(x, core) + place(core) + place(1 - core)
    for v in (z_low, y):
        values += listed(v, core) + listed(v, 1 - core)
    return jnp.stack(values).astype(jnp.int32)


def conv_whole(track, edges, weight_a, weight_b, out, flat, shifted):
    for i in range(0, 384, 48):
        rows = gelu_rows(track[i : i + 48, :]).astype(jnp.bfloat16).astype(jnp.float32)
        for c in range(10):
            flat[c, 8 + i : 56 + i, :] = rows[:, c * 128 : (c + 1) * 128]
    shift_rows(3, None, edges, flat, shifted)
    out[:, 0:192] = conv_tile(shifted, weight_a)
    out[:, 192:384] = conv_tile(shifted, weight_b)


CONV_SCRATCH = (pltpu.VMEM((10, 400, 128), jnp.float32), pltpu.VMEM((1152, 1280), jnp.bfloat16))


def conv_a(place, act, edges, weight):
    body = functools.partial(conv_first, place)
    return call(body, bf16(192, 192), CONV_SCRATCH, 0, "conv_a")(act, edges, weight)


def conv_b(place, act, edges, weight, first):
    body = functools.partial(conv_second, place)
    return call(body, bf16(192, 384), CONV_SCRATCH, 0, "conv_b")(act, edges, weight, first)


def conv_far(track, edges, weight_a, weight_b):
    return call(conv_whole, bf16(192, 384), CONV_SCRATCH, 0, "conv_far")(track, edges, weight_a, weight_b)


def smem():
    return pl.BlockSpec(memory_space=pltpu.SMEM)


def vmem():
    return pl.BlockSpec(memory_space=pltpu.VMEM)


def place_kernel(spots, own0, own1, sib0, sib1, out, rows):
    core = spots[1]
    for side, pair in enumerate(((own0, own1), (sib0, sib1))):
        which = (core + side) % 2
        for r in range(4):
            quarter = spots[22 + 4 * side + r]
            rows[which * 4 + quarter] = pair[r // 2][r % 2]
    for c in range(2):
        whole = jnp.concatenate([rows[c * 4 + q] for q in range(4)], axis=0)
        for k in range(5):
            out[k, c * 96 : (c + 1) * 96, :] = whole[k * 96 : (k + 1) * 96]


def place(spots, own, sibling):
    return call(
        place_kernel,
        bf16(5, 192, 1280),
        (pltpu.VMEM((8, 120, 1280), jnp.bfloat16),),
        0,
        "place",
        [smem()] + [vmem()] * 4,
    )(spots, *own, *sibling)


def sort_kernel(spots, types, q, o):
    for t in range(8):
        place, zh = spots[6 + t % 4], t // 4
        q[t] = types[place, zh * 96 : zh * 96 + 96, :]
        o[t] = types[place, 192 + zh * 96 : 288 + zh * 96, :]


def sort(spots, types):
    return call(
        sort_kernel,
        (bf16(8, 96, 384), bf16(8, 96, 384)),
        name="sort",
        specs=[smem(), vmem()],
    )(spots, types)


def shards_columns(spots, base, columns, pairs, blocks):
    for side in range(2):
        count = pairs[side][0].shape[1]
        total = jnp.zeros((count * 96, 192), jnp.float32)
        for r in range(4):
            weight = pairs[side][r // 2][r % 2].reshape(count * 96, 384)
            total = total + lax.dot_general(
                weight, columns[spots[base + 4 * side + r]], NT, preferred_element_type=jnp.float32
            )
        for t in range(count):
            blocks[2 * t + (spots[1] + side) % 2] = total[t * 96 : t * 96 + 96, :]


def key_value_kernel(spots, p0, p1, p2, p3, a0, a1, b0, b1, pooled, columns, kv, rest, tiles, blocks, wide):
    zh = spots[0]
    for s, piece in enumerate((p0, p1, p2, p3)):
        home = spots[2 + s]
        tiles[zh * 4 + home] = piece[:, 0:192]
        tiles[(1 - zh) * 4 + home] = piece[:, 192:384]
    for i in range(8):
        pooled[:, i * 192 : i * 192 + 192] = tiles[i]
    normed = rms_scaled(pooled[...].astype(jnp.float32)).astype(jnp.bfloat16)
    for i in range(4):
        columns[i] = normed[:, i * 384 : i * 384 + 384]
    shards_columns(spots, 14, columns, ((a0, a1), (b0, b1)), blocks)
    wide[0:68, :] = blocks[0, 16:84]
    for i in range(1, 4):
        wide[i * 84 - 16 : i * 84 + 68, :] = blocks[i, 0:84]
    wide[320:336, :] = blocks[0, 0:16]
    wide[336:384, :] = jnp.zeros((48, 192), jnp.float32)
    rows = jnp.transpose(wide[...]).astype(jnp.bfloat16)
    kv[...] = rows[:, 0:320]
    rest[...] = rows[:, 256:384]


def key_value(spots, tiles, own, sibling):
    return call(
        key_value_kernel,
        (bf16(192, 1536), bf16(4, 192, 384), bf16(192, 320), bf16(192, 128)),
        (
            pltpu.VMEM((8, 192, 192), jnp.bfloat16),
            pltpu.VMEM((4, 96, 192), jnp.float32),
            pltpu.VMEM((384, 192), jnp.float32),
        ),
        name="key_value",
        specs=[smem()] + [vmem()] * 8,
    )(spots, *tiles, *own, *sibling)


def query_kernel(spots, columns, rest, a0, a1, b0, b1, q, blocks, wide):
    shards_columns(spots, 14, columns, ((a0, a1), (b0, b1)), blocks)
    for i in range(12):
        wide[i * 84 : i * 84 + 84, :] = blocks[i, 0:84]
    q[:, 0:896] = jnp.transpose(wide[0:896, :]).astype(jnp.bfloat16)
    last = jnp.concatenate([jnp.transpose(wide[896:1024, :])[:, 0:112], rest[:, 64:80].astype(jnp.float32)], axis=1)
    q[:, 896:1024] = last.astype(jnp.bfloat16)


def query(spots, columns, rest, own, sibling):
    return call(
        query_kernel,
        bf16(192, 1024),
        (pltpu.VMEM((12, 96, 192), jnp.float32), pltpu.VMEM((1024, 192), jnp.float32)),
        name="query",
        specs=[smem()] + [vmem()] * 6,
    )(spots, columns, rest, *own, *sibling)


SCALE = QK ** (-0.5) * 1.4426950408889634


def attend(q, own, sibling, h, state):
    query = q[:, h * QK : (h + 1) * QK]
    blocks = [own[...].reshape(768, 320), sibling[...].reshape(768, 320)]
    scores = [
        lax.dot_general(query, b[:, 0:QK], NT, preferred_element_type=jnp.float32) for b in blocks
    ]
    top = jnp.maximum(
        jnp.max(scores[0], axis=1, keepdims=True), jnp.max(scores[1], axis=1, keepdims=True)
    )
    if state is not None:
        top = jnp.maximum(top, state[0])
    shift = top * SCALE
    expo = [jnp.exp2(s * SCALE - shift) for s in scores]
    total = jnp.sum(expo[0], axis=1, keepdims=True) + jnp.sum(expo[1], axis=1, keepdims=True)
    value = jnp.dot(expo[0].astype(jnp.bfloat16), blocks[0][:, QK:], preferred_element_type=jnp.float32)
    value = value + jnp.dot(
        expo[1].astype(jnp.bfloat16), blocks[1][:, QK:], preferred_element_type=jnp.float32
    )
    if state is not None:
        factor = jnp.exp2(state[0] * SCALE - shift)
        total = total + state[1] * factor
        value = value + state[2] * factor
    return top, total, value


def attend_first(q, own, sibling, top_out, total_out, value_out):
    for h in range(HEADS):
        top, total, value = attend(q, own, sibling, h, None)
        top_out[:, h : h + 1] = top
        total_out[:, h : h + 1] = total
        value_out[h] = value


def attend_second(q, own, sibling, top_in, total_in, value_in, heads):
    for h in range(HEADS):
        state = (top_in[:, h : h + 1], total_in[:, h : h + 1], value_in[h])
        top, total, value = attend(q, own, sibling, h, state)
        heads[:, h * VD : (h + 1) * VD] = (value / total).astype(jnp.bfloat16)


def output_kernel(spots, heads, pooled, a0, a1, b0, b1, mixed, columns, blocks):
    for i in range(4):
        columns[i] = heads[:, i * 384 : i * 384 + 384]
    shards_columns(spots, 22, columns, ((a0, a1), (b0, b1)), blocks)
    for i in range(4):
        cols = slice(i * 384, i * 384 + 384)
        part = jnp.transpose(blocks[i * 4 : i * 4 + 4].reshape(384, 192))
        mixed[:, cols] = (pooled[:, cols].astype(jnp.float32) + part).astype(jnp.bfloat16)


def output(spots, heads, pooled, own, sibling):
    return call(
        output_kernel,
        bf16(192, 1536),
        (
            pltpu.VMEM((4, 192, 384), jnp.bfloat16),
            pltpu.VMEM((16, 96, 192), jnp.float32),
        ),
        2 * 192 * 1536 * 1536,
        "output",
        [smem()] + [vmem()] * 6,
    )(spots, heads, pooled, *own, *sibling)


def first(core):
    return 1 + 2 * core


def second(core):
    return 3 - 2 * core


def swap(value):
    return send(value, lambda x, y, z, c: (x, y, z, 1 - c))


def swapped(pairs):
    return swap(pairs[0]), swap(pairs[1])


def after(gate, *values):
    held = lax.optimization_barrier((*values, *gate))
    return held[0] if len(values) == 1 else held[: len(values)]


def to_first(value):
    return send(value, lambda x, y, z, c: (x ^ first(c), y, z, c))


def to_second(value):
    return send(value, lambda x, y, z, c: (x ^ second(c), y, z, c))


def to_far(value):
    return send(value, lambda x, y, z, c: (x ^ 2, y, z, c))


def across(value):
    return send(value, lambda x, y, z, c: (x, y, z + 4, c))


def x_pair(value):
    return jnp.stack([value, to_first(value)])


def x_four(pair):
    return jnp.concatenate([pair, to_second(pair)], axis=0)


def y_first(value):
    return value, send(value, lambda x, y, z, c: (x, y ^ first(c), z, c))


def y_second(pair):
    return pair, send(pair, lambda x, y, z, c: (x, y ^ second(c), z, c))


def z_step(z, c):
    return z ^ 1 if c == 0 else z + 2 * (z % 2) - 1


def z_first(value):
    return value, send(value, lambda x, y, z, c: (x, y, z_step(z, c), c))


def z_second(pair):
    return pair, send(pair, lambda x, y, z, c: (x, y, z_step(z, 1 - c), c))


def on_device(track, conv_weight, qkv_weight, out_weight):
    dp = lax.axis_index("dp")
    seq = lax.axis_index("seq")
    x, y, z_low, zh, core = (seq // 2) % 4, dp % 4, dp // 4, seq // 8, seq % 2
    spots = spots_of(x, y, z_low, zh, core)

    own = jnp.transpose(conv_weight, (1, 0, 2)).reshape(480, 1280)
    packed = pack(spots, own.reshape(4, 120, 1280), qkv_weight, out_weight)
    top = lax.ppermute(track[376:384], "seq", [(i, i + 1) for i in range(15)])
    bottom = lax.ppermute(track[0:8], "seq", [(i + 1, i) for i in range(15)])
    crossed = across(packed)
    near, beside = to_first(track), to_second(track)

    def unfold(rows):
        return jnp.concatenate([rows[:, i * 384 : i * 384 + 384] for i in range(3)], axis=0)

    def both(rows):
        pair = [unfold(packed[rows]), unfold(crossed[rows])]
        return jnp.where(zh == 0, jnp.stack(pair), jnp.stack(pair[::-1]))

    types = [both(rows).reshape(192, 384) for rows in (slice(0, 32), slice(32, 64))]
    sibling = swap(own)
    low = jnp.where(core == 0, own, sibling).reshape(5, 96, 1280)
    high = jnp.where(core == 0, sibling, own).reshape(5, 96, 1280)
    weight_a = jnp.concatenate([low, high], axis=1)

    near, beside, top, bottom, conv_crossed, *types = after(
        (), near, beside, top, bottom, crossed[64:184], *types
    )
    edges = x_pair(jnp.concatenate([top, bottom], axis=0))
    all_edges = x_four(edges)
    types = x_four(x_pair(jnp.concatenate(types, axis=0)))
    far = to_second(near)
    others = jnp.stack(y_first(conv_crossed))
    others_sibling = swap(others)
    others_far = y_second(others)[1]

    q_types, o_types = sort(spots, types)
    q_near = z_first(q_types)[1]
    act, near, beside = gelu(track), gelu(near), gelu(beside)
    first_own, first_near = conv_a(0, act, edges, weight_a), conv_a(1, near, edges, weight_a)
    all_edges = after((first_own, first_near), all_edges)
    first_beside = conv_a(2, beside, all_edges, weight_a)
    weight_b = place(spots, (others, others_far), (others_sibling, swap(others_far)))
    weight_b = after((first_own, first_near, first_beside), weight_b)
    o_own = y_first(o_types)

    tile_near = conv_b(1, near, edges, weight_b, first_near)
    from_near = to_first(tile_near)
    far, q_near = after((tile_near,), far, q_near)
    kv_own = z_second(jnp.stack([q_types[6:8], q_near[6:8]]))
    tile_far = conv_far(far, all_edges, weight_a, weight_b)
    from_far = to_far(tile_far)
    tile_beside = conv_b(2, after((tile_far,), beside), all_edges, weight_b, first_beside)
    from_beside = to_second(tile_beside)
    gate = (tile_beside, from_near, from_far, *kv_own)
    act, q_types, q_near, *kv_own = after(gate, act, q_types, q_near, *kv_own)
    kv_sibling = swapped(kv_own)
    q_own = z_second(jnp.stack([q_types[0:6], q_near[0:6]]))
    tile_own = conv_b(0, act, edges, weight_b, first_own)
    tiles = [tile_own, from_near, from_beside, from_far]

    pooled, columns, kv, rest = key_value(spots, tiles, kv_own, kv_sibling)

    def spread(block):
        return [block, to_first(block), to_second(block), to_far(block)]

    q_far = after((kv,), q_own[1])
    o_own = y_second(jnp.stack(after((kv,), *o_own)))
    q_own, q_sibling = (q_own[0], q_far), (swap(after((tile_far,), q_own[0])), swap(q_far))
    queries = query(spots, columns, rest, q_own, q_sibling)
    kv_cross, *near_own, queries, o_far = after((), across(kv), *spread(kv), queries, o_own[1])
    near_own = jnp.stack(near_own)
    near_sibling = swap(near_own)
    far_own = spread(kv_cross)
    state = call(
        attend_first, (f32(192, 8), f32(192, 8), f32(8, 192, 192)), name="attend_first"
    )(queries, near_own, near_sibling)
    far_own = jnp.stack(after((state[0],), *far_own))
    far_sibling = swap(far_own)
    o_own = o_own[0], o_far
    o_sibling = swapped(after((queries,), *o_own))
    heads = call(attend_second, bf16(192, 1536), name="attend_second")(
        queries, far_own, far_sibling, *state
    )
    return output(spots, heads, pooled, o_own, o_sibling)


def solution(mesh):
    return jax.shard_map(
        on_device,
        mesh=mesh,
        in_specs=(P(("dp", "seq"), None), P("seq", None, None), P("seq", None), P("seq", None)),
        out_specs=P(("dp", "seq"), None),
        check_vma=False,
    )
```
